256 devices in a mesh: fsdp: 32 (over y, z), tp: 8 (over x, core).
Axes of the slice: x: 4, y: 4, z: 8, core: 2. Of those that a mesh axis runs over, the one named last changes fastest.
Arguments:
- gradient: bfloat16 [256, 1024, 1024], P('tp', 'fsdp'), may hold values from -700 to 700
- slot_ids: int32 [256], P('tp'), may hold values from 0 to 63, as said below
- left_root: bfloat16 [512, 1024, 1024], P(('fsdp', 'tp')), may hold values from -0.1 to 4, as said below
- right_root: bfloat16 [512, 1024, 1024], P(('fsdp', 'tp')), may hold values from -0.1 to 4, as said below
Outputs:
- update: bfloat16 [256, 1024, 1024], P('tp', 'fsdp')
The draws below stay inside these ranges and needn't reach their ends.
Inputs may be any that keep to these rules, and one draw needn't show every extreme that they name: `slot_ids`: blocks 32 * t to 32 * t + 31 form group t; within a group no two blocks share a value; value v names slot v % 2 of fsdp index v // 2; in every group some fsdp index receives 2 blocks. `left_root`: Symmetric, with the largest entries on the diagonal. `right_root`: Symmetric, with the largest entries on the diagonal.
All inputs are finite; a program needn't handle non-finite values.
Results may differ from the reference program's by a relative error of at most 0.0057.
Values may be sent and summed in bfloat16 or wider, within the bound.
A program may use at most 192 MiB of HBM per device.

```python
import math
import jax
import jax.numpy as jnp
from jax import lax

BS = 1024
OWN_MAX = 2
GROUP = 32
NBLOCKS = 256
SLOT_IDS = 64
SLOTS_ALL = 512
N_TP = 8


def rooted_slots(key, lowest, highest):

    def one_slot(which):
        slot_key = jax.random.fold_in(key, which)
        k_gauss = jax.random.fold_in(slot_key, 0)
        k_diag = jax.random.fold_in(slot_key, 2)
        gauss = jnp.clip(jax.random.normal(k_gauss, (BS, BS), jnp.float32), -1.7, 1.7)
        noise = gauss
        sym = (noise + noise.T) * (0.3 / math.sqrt(2.0 * BS))
        diag = jnp.exp(jax.random.uniform(k_diag, (BS,), jnp.float32, math.log(lowest), math.log(highest)))
        eye = jnp.eye(BS, dtype=jnp.float32)
        return (sym * (1.0 - eye) + eye * diag[None, :]).astype(jnp.bfloat16)
    return lax.map(one_slot, jnp.arange(SLOTS_ALL, dtype=jnp.int32))


def draw_left_root(key, part):
    key = jax.random.fold_in(key, 21)
    return rooted_slots(key, 0.8, 3.0)


def draw_right_root(key, part):
    key = jax.random.fold_in(key, 37)
    return rooted_slots(key, 0.8, 3.0)


def draw_gradient(key, part):
    key = jax.random.fold_in(key, 11)
    k_base, k_rows, k_cols = jax.random.split(key, 3)
    row_pos = jnp.arange(BS, dtype=jnp.float32)[None, :, None] / BS
    row_scale = jnp.exp(jax.random.uniform(k_rows, (NBLOCKS, BS, 1), jnp.float32) * math.log(10.0))
    col_scale = jnp.exp(jax.random.uniform(k_cols, (NBLOCKS, 1, BS), jnp.float32) * math.log(10.0))
    base = jnp.clip(jax.random.normal(k_base, (NBLOCKS, BS, BS), jnp.float32), -4.0, 4.0)
    rise = jnp.sqrt(1.0 + 2.0 * row_pos)
    return (base * row_scale * col_scale * rise).astype(jnp.bfloat16)


def draw_slot_ids(key, part):
    key = jax.random.fold_in(key, 5)

    def one_group(group_key):
        k_score, k_forced, k_order = jax.random.split(group_key, 3)
        numbers = jnp.arange(SLOT_IDS, dtype=jnp.int32)
        score = jax.random.randint(k_score, (SLOT_IDS,), 0, 2 ** 20, dtype=jnp.int32)
        forced = jax.random.randint(k_forced, (), 0, SLOT_IDS // OWN_MAX, dtype=jnp.int32)
        score = score * SLOT_IDS + numbers + jnp.where(numbers // OWN_MAX == forced, 2 ** 21 * SLOT_IDS, 0).astype(jnp.int32)
        unused, chosen = lax.top_k(score, GROUP)
        order = jax.random.permutation(k_order, GROUP)
        return chosen[order].astype(jnp.int32)
    keys = jax.random.split(key, N_TP)
    return jax.vmap(one_group)(keys).reshape(NBLOCKS).astype(jnp.int32)


def setup_inputs(seed: int = 0) -> dict:
    seeds = jax.random.split(jax.random.key(seed), 5)
    return {
        "gradient": draw_gradient(jax.random.fold_in(seeds[4], 71), 0),
        "slot_ids": draw_slot_ids(jax.random.fold_in(seeds[4], 71), 0),
        "left_root": draw_left_root(jax.random.fold_in(seeds[4], 71), 0),
        "right_root": draw_right_root(jax.random.fold_in(seeds[4], 71), 0),
    }


def reference(gradient, slot_ids, left_root, right_root):
    blocks = jnp.arange(NBLOCKS, dtype=jnp.int32)
    group = blocks // GROUP
    index = (slot_ids // OWN_MAX * N_TP + group) * OWN_MAX + slot_ids % OWN_MAX
    index = index.astype(jnp.int32)

    def precondition(pair):
        grad_block, where = pair
        left = lax.dynamic_index_in_dim(left_root, where, 0, keepdims=False)
        right = lax.dynamic_index_in_dim(right_root, where, 0, keepdims=False)
        inner = jnp.dot(left, grad_block, preferred_element_type=jnp.float32).astype(jnp.bfloat16)
        return jnp.dot(inner, right, preferred_element_type=jnp.float32).astype(jnp.bfloat16)
    direction = lax.map(precondition, (gradient, index))
    wide = direction.astype(jnp.float32)
    total = jnp.sum(wide * wide)
    factor = 0.5 / jnp.sqrt(total / (NBLOCKS * BS * BS) + 1e-06)
    return (wide * factor).astype(jnp.bfloat16)
```

```python
import jax
import jax.numpy as jnp
from jax import lax
from jax.experimental import pallas as pl
from jax.experimental.pallas import tpu as pltpu
from jax.sharding import PartitionSpec as P

MESH = pl.DeviceIdType.MESH
NF = 32
NZ = 8
NY = 4
NT = 8
BLOCKS = 32
ROWS = 32
W = 1024
CW = 128
SECONDS = 16
LIST = 16
BAND = 256
HALF = 16
PAIRS = NT * NY
EARLY, MIDDLE = 6, 12

BF16 = jnp.bfloat16
F32 = jnp.float32
I32 = jnp.int32

FIRST, IDS, SUM_F, SUM_T = 0, 1, 2, 3
BACK_FIRST, SPREAD, CROSS, COLLECT, BACK_COLLECT, BACK_CROSS, BACK_SPREAD, N_SEMS = range(4, 20, 2)
GRAD, LEFT, RIGHT, TAB_A, TAB_B, OUT, OWN, N_LOCAL = range(8)
T_FIRST, T_SEL, T_HAS1, T_HAS2, T_RANK, T_PLACE, T_SECOND, T_BACK, T_CROSS, T_RETURN, N_TABS = range(11)


def dot(a, b):
    return jnp.dot(a, b, preferred_element_type=F32)


def within(index, size):
    return jnp.clip(index, 0, size - 1)


def owners(ids):
    lane = lax.broadcasted_iota(I32, (8, 128), 1)
    zero = jnp.zeros((8, 128), F32)
    p0, p1, b0, b1 = zero, zero, zero, zero
    for b in range(BLOCKS):
        column = jnp.broadcast_to(ids[:, b : b + 1], (8, 128))
        e0 = jnp.where(column == 2 * lane, 1.0, 0.0)
        e1 = jnp.where(column == 2 * lane + 1, 1.0, 0.0)
        p0, p1 = jnp.maximum(p0, e0), jnp.maximum(p1, e1)
        b0, b1 = b0 + b * e0, b1 + b * e1
    has2 = p0 * p1
    earlier = lax.broadcasted_iota(I32, (128, 128), 0) < lax.broadcasted_iota(I32, (128, 128), 1)
    rank = dot(has2.astype(BF16), jnp.where(earlier, 1.0, 0.0).astype(BF16))
    first = jnp.clip(p0 * b0 + (1.0 - p0) * b1, 0.0, BLOCKS - 1.0)
    return p0, p1, first, b1, has2, rank


def by_rank(has2, rank, value, highest):
    lane = lax.broadcasted_iota(I32, (8, 128), 1)
    table = jnp.zeros((8, 128), F32)
    for j in range(SECONDS):
        found = jnp.sum(jnp.where(rank == float(j), has2 * value, 0.0), axis=1, keepdims=True)
        table = jnp.where(lane == j, jnp.broadcast_to(found, (8, 128)), table)
    return jnp.clip(table, 0.0, float(highest)).astype(I32)


def by_place(has2, place, value, highest):
    row = lax.broadcasted_iota(I32, (16, 128), 0)
    rows = jnp.zeros((16, 128), F32)
    for i in range(LIST):
        found = jnp.sum(jnp.where(place == float(i), has2 * value, 0.0), axis=0, keepdims=True)
        rows = jnp.where(row == i, jnp.broadcast_to(found, (16, 128)), rows)
    source = lax.broadcasted_iota(I32, (128, 128), 0)
    target = lax.broadcasted_iota(I32, (128, 128), 1)
    fold = jnp.where((source % NZ == target) & (source < NF), 1.0, 0.0).astype(BF16)
    return jnp.clip(dot(rows.astype(BF16), fold), 0.0, float(highest)).astype(I32)


def kernel(
    ids_ref, ids_smem, grad_hbm, left_hbm, right_hbm, out_hbm, flag_ref,
    grad, left, right, snd0, rcv0, sp_snd, sp_rcv, z_snd, z_rcv, c_snd, rcv1, inner, dir0, dir1,
    ret0, rc, rz_snd, rz_rcv, rs_snd, rs_rcv, outv, ids_snd, ids_all, tab_a, tab_b, tab_as, tab_bs,
    part_f, part_t, sum_f, sum_t, ss, rs, ls,
):
    f = lax.axis_index("fsdp")
    t = lax.axis_index("tp")
    y, z = f // NZ, f % NZ

    def shifted(k):
        return lax.rem(y + k // NZ, NY) * NZ + lax.rem(z + lax.rem(k, NZ), NZ)

    def tp_shifted(k):
        return lax.rem(t + k, NT)

    def z_shifted(k):
        return lax.rem(z + k, NZ)

    def send(source, target, phase, to_f, to_t):
        pltpu.make_async_remote_copy(
            src_ref=source, dst_ref=target, send_sem=ss.at[phase], recv_sem=rs.at[phase],
            device_id=(to_f, to_t), device_id_type=MESH,
        ).start()

    def own(source, target, phase):
        pltpu.make_async_copy(source, target, rs.at[phase]).start()

    def wait(ref, sem):
        pltpu.make_async_copy(ref, ref, sem).wait()

    def loop(lowest, highest, body):
        def step(k, carry):
            body(k)
            return carry

        lax.fori_loop(lowest, highest, step, 0)

    load_grad = pltpu.make_async_copy(grad_hbm, grad, ls.at[GRAD])
    load_left = pltpu.make_async_copy(left_hbm, left, ls.at[LEFT])
    load_right = pltpu.make_async_copy(right_hbm, right, ls.at[RIGHT])
    load_grad.start()

    barrier = pltpu.get_barrier_semaphore()

    def greet_f(k):
        pl.semaphore_signal(barrier, inc=1, device_id=(shifted(k), t), device_id_type=MESH)

    def greet_t(k):
        pl.semaphore_signal(
            barrier, inc=1, device_id=(lax.rem(y + lax.rem(k, NY), NY) * NZ + z, tp_shifted(k // NY)), device_id_type=MESH
        )

    loop(1, NF, greet_f)
    loop(NY, PAIRS, greet_t)
    load_left.start()
    load_right.start()

    ids_snd[...] = jnp.full((8, 128), -1, I32)
    ids_snd[:, :BLOCKS] = jnp.broadcast_to(ids_ref[...], (8, BLOCKS))
    p0, p1, first, second, has2, rank = owners(ids_snd[...])
    tab_a[0] = first.astype(I32)
    tab_a[1] = by_rank(has2, rank, second, BLOCKS - 1)
    copy_a = pltpu.make_async_copy(tab_a, tab_as, ls.at[TAB_A])
    copy_a.start()
    ids_all[t] = ids_snd[...]
    pl.semaphore_wait(barrier, NF - 1 + PAIRS - NY)

    def send_ids(k):
        send(ids_snd, ids_all.at[t], IDS, f, tp_shifted(k))

    loop(1, NT, send_ids)
    copy_a.wait()
    load_grad.wait()

    def pack_spread(j):
        b = within(tab_as[1, 0, j], BLOCKS)
        for h in range(2):
            for r in range(NT):
                sp_snd[h][r * SECONDS + j] = grad[b, h * HALF : (h + 1) * HALF, r * CW : (r + 1) * CW]

    def spread(source, target, phase, h):
        def one(k):
            to = tp_shifted(k)
            send(source[h].at[pl.ds(to * SECONDS, SECONDS)], target[h].at[pl.ds(t * SECONDS, SECONDS)], phase + h, f, to)

        loop(1, NT, one)
        mine = pl.ds(t * SECONDS, SECONDS)
        own(source[h].at[mine], target[h].at[mine], phase + h)

    def cross(source, target, phase, h):
        def one(k):
            to = z_shifted(k)
            send(source[h].at[pl.ds(to * LIST, LIST)], target[h].at[pl.ds(z * LIST, LIST)], phase + h, y * NZ + to, t)

        loop(1, NZ, one)
        mine = pl.ds(z * LIST, LIST)
        own(source[h].at[mine], target[h].at[mine], phase + h)

    loop(0, SECONDS, pack_spread)
    spread(sp_snd, sp_rcv, SPREAD, 0)
    spread(sp_snd, sp_rcv, SPREAD, 1)

    def send_first(k):
        to = shifted(k)
        snd0[to] = grad[within(tab_as[0, 0, to], BLOCKS)]
        send(snd0.at[to], rcv0.at[pl.ds(f * ROWS, ROWS)], FIRST, to, t)

    loop(1, EARLY, send_first)

    wait(ids_all.at[pl.ds(0, NT - 1)], rs.at[IDS])
    row = lax.broadcasted_iota(I32, (8, 128), 0)
    ids = jnp.zeros((8, 128), I32)
    for g in range(NT):
        ids = jnp.where(row == g, ids_all[g], ids)
    p0, p1, first, second, has2, rank = owners(ids)
    source = lax.broadcasted_iota(I32, (128, 128), 0)
    target = lax.broadcasted_iota(I32, (128, 128), 1)
    plane = jnp.where((source % NZ == target % NZ) & (source < NF), 1.0, 0.0)
    before = jnp.where(source // NZ < target // NZ, plane, 0.0)
    in_plane = dot(has2.astype(BF16), plane.astype(BF16))
    place = dot(has2.astype(BF16), before.astype(BF16))
    for g in range(NT - 1):
        place = place + jnp.where(row > g, jnp.broadcast_to(in_plane[g : g + 1, :], (8, 128)), 0.0)
    longest = jnp.max(jnp.sum(in_plane, axis=0, keepdims=True), axis=1, keepdims=True)
    flag_ref[0, 0] = jnp.max(longest.astype(I32))
    bounded = jnp.clip(place, 0.0, LIST - 1.0)
    group = row.astype(F32)
    lane = lax.broadcasted_iota(I32, (8, 128), 1)
    tab_b[...] = jnp.zeros_like(tab_b)
    tab_b[T_SEL, :8] = (1.0 - p0).astype(I32)
    tab_b[T_HAS1, :8] = jnp.maximum(p0, p1).astype(I32)
    tab_b[T_HAS2, :8] = has2.astype(I32)
    tab_b[T_RANK, :8] = jnp.clip(rank, 0.0, SECONDS - 1.0).astype(I32)
    tab_b[T_PLACE, :8] = bounded.astype(I32)
    tab_b[T_BACK, :8] = by_rank(has2, rank, (lane % NZ).astype(F32) * LIST + bounded, NZ * LIST - 1)
    tab_b[T_CROSS] = by_place(has2, place, group * SECONDS + rank, NT * SECONDS - 1)
    tab_b[T_RETURN] = by_place(has2, place, group * NY + (lane // NZ).astype(F32), PAIRS - 1)
    copy_b = pltpu.make_async_copy(tab_b, tab_bs, ls.at[TAB_B])
    copy_b.start()
    copy_b.wait()

    def pack_cross(h):
        def one(k):
            z_snd[h][k] = sp_rcv[h][within(tab_bs[T_CROSS, k % LIST, k // LIST], NT * SECONDS)]

        loop(0, NZ * LIST, one)

    for h, lowest, highest in ((0, EARLY, MIDDLE), (1, MIDDLE, NF)):
        wait(sp_rcv[h], rs.at[SPREAD + h])
        pack_cross(h)
        cross(z_snd, z_rcv, CROSS, h)
        loop(lowest, highest, send_first)
    snd0[f] = grad[within(tab_as[0, 0, f], BLOCKS)]
    own(snd0.at[f], rcv0.at[pl.ds(f * ROWS, ROWS)], FIRST)

    here = t * NY + y

    def pack_collect(h):
        def one(q):
            place_q = within(tab_bs[T_PLACE, q // NY, (q % NY) * NZ + z], LIST)
            for s in range(NZ):
                c_snd[h][q, s] = z_rcv[h][s * LIST + place_q]

        loop(0, PAIRS, one)

    def collect(h):
        def one(k):
            to_t, to_y = tp_shifted(k // NY), lax.rem(y + lax.rem(k, NY), NY)
            send(c_snd[h].at[to_t * NY + to_y], rcv1.at[t, pl.ds(y * NZ, NZ), h], COLLECT + h, to_y * NZ + z, to_t)

        loop(1, PAIRS, one)
        own(c_snd[h].at[here], rcv1.at[t, pl.ds(y * NZ, NZ), h], COLLECT + h)

    for h in range(2):
        wait(z_rcv[h], rs.at[CROSS + h])
        pack_collect(h)
        collect(h)

    load_left.wait()
    load_right.wait()
    wait(rcv1.at[:, :, 0], rs.at[COLLECT])
    wait(rcv1.at[:, :, 1], rs.at[COLLECT + 1])

    def squares(total, part):
        wide = part.astype(F32)
        return total + jnp.sum((wide * wide).reshape(BAND // 8, 8, BAND), axis=0)

    def back_collect(to_y, to_t, h):
        send(dir1.at[to_t, pl.ds(to_y * NZ, NZ), h], rc[h].at[here], BACK_COLLECT + h, to_y * NZ + z, to_t)

    def second_band(k, total):
        to_y = lax.rem(y + k, NY)
        rows = pl.ds(to_y * BAND, BAND)
        lhs = left[1, rows, :]
        for c in range(W // BAND):
            rhs = jnp.concatenate([rcv1[2 * c].reshape(W, CW), rcv1[2 * c + 1].reshape(W, CW)], axis=1)
            inner[:, c * BAND : (c + 1) * BAND] = dot(lhs, rhs).astype(BF16)
        mid = inner[...]
        for c in range(W // BAND):
            part = dot(mid, right[1, :, c * BAND : (c + 1) * BAND]).astype(BF16)
            for i in range(2):
                dir1[2 * c + i, pl.ds(to_y * NZ, NZ)] = part[:, i * CW : (i + 1) * CW].reshape(NZ, 2, HALF, CW)
            total = squares(total, part)
        loop(jnp.where(k == 0, 1, 0), NT, lambda r: back_collect(to_y, tp_shifted(r), 0))
        return total

    zeros = jnp.zeros((8, BAND), F32)
    sum1 = lax.fori_loop(0, NY, second_band, zeros)
    loop(1, PAIRS, lambda k: back_collect(lax.rem(y + lax.rem(k, NY), NY), tp_shifted(k // NY), 1))
    for h in range(2):
        own(dir1.at[t, pl.ds(y * NZ, NZ), h], rc[h].at[here], BACK_COLLECT + h)

    wait(rcv0, rs.at[FIRST])
    which = within(tab_bs[T_SEL, t, f], 2)

    def back_first(k, h):
        to = shifted(k)
        send(dir0.at[pl.ds(to * ROWS + h * HALF, HALF)], ret0[h].at[f], BACK_FIRST + h, to, t)

    def first_band(k, total):
        rows = pl.ds(lax.rem(y + k, NY) * BAND, BAND)
        lhs = left[which, rows, :]
        for c in range(W // BAND):
            inner[:, c * BAND : (c + 1) * BAND] = dot(lhs, rcv0[:, c * BAND : (c + 1) * BAND]).astype(BF16)
        mid = inner[...]
        for c in range(W // BAND):
            part = dot(mid, right[which, :, c * BAND : (c + 1) * BAND]).astype(BF16)
            dir0[rows, c * BAND : (c + 1) * BAND] = part
            total = squares(total, part)
        loop(jnp.where(k == 0, 1, 0), NZ, lambda s: back_first(k * NZ + s, 0))
        return total

    sum0 = lax.fori_loop(0, NY, first_band, zeros)
    for h in range(2):
        own(dir0.at[pl.ds(f * ROWS + h * HALF, HALF)], ret0[h].at[f], BACK_FIRST + h)

    kept = jnp.where(tab_bs[T_HAS1, t, f] > 0, sum0, 0.0) + jnp.where(tab_bs[T_HAS2, t, f] > 0, sum1, 0.0)
    part_f[...] = kept[:, :128] + kept[:, 128:]
    sum_f[f] = part_f[...]
    loop(1, NF, lambda k: send(part_f, sum_f.at[f], SUM_F, shifted(k), t))

    def pack_back_cross(h):
        def one(k):
            rz_snd[h][k] = rc[h][within(tab_bs[T_RETURN, k % LIST, z], PAIRS), k // LIST]

        loop(0, NZ * LIST, one)

    for h in range(2):
        wait(rc[h], rs.at[BACK_COLLECT + h])
        pack_back_cross(h)
        cross(rz_snd, rz_rcv, BACK_CROSS, h)

    loop(1, NF, lambda k: back_first(k, 1))

    wait(sum_f.at[pl.ds(0, NF - 1)], rs.at[SUM_F])
    part_t[...] = jnp.sum(sum_f[...], axis=0)
    sum_t[t] = part_t[...]
    loop(1, NT, lambda k: send(part_t, sum_t.at[t], SUM_T, f, tp_shifted(k)))

    def pack_back_spread(h):
        def one(k):
            rs_snd[h][k] = rz_rcv[h][within(tab_bs[T_BACK, k // SECONDS, k % SECONDS], NZ * LIST)]

        loop(0, NT * SECONDS, one)

    for h in range(2):
        wait(rz_rcv[h], rs.at[BACK_CROSS + h])
        pack_back_spread(h)
        spread(rs_snd, rs_rcv, BACK_SPREAD, h)

    wait(sum_t.at[pl.ds(0, NT - 1)], rs.at[SUM_T])
    total = jnp.full((8, 128), jnp.sum(jnp.sum(sum_t[...], axis=0)))
    factor = 0.5 / jnp.sqrt(total / float(NT * BLOCKS * W * W) + 1e-6)
    scale = jnp.broadcast_to(factor[:1, :], (HALF, CW))

    def finish(h):
        def one(b):
            v = within(ids_smem[b], 2 * NF)
            o = v // 2
            is_second = (v % 2) * tab_bs[T_HAS2, t, o]
            j = within(is_second * tab_bs[T_RANK, t, o], SECONDS)
            rows = slice(h * HALF, (h + 1) * HALF)
            for r in range(NT):
                columns = slice(r * CW, (r + 1) * CW)
                value = jnp.where(is_second > 0, rs_rcv[h][r * SECONDS + j], ret0[h][o, :, columns])
                outv[b, rows, columns] = (value.astype(F32) * scale).astype(BF16)
            pltpu.make_async_copy(outv.at[b, rows], out_hbm.at[b, rows], ls.at[OUT]).start()

        loop(0, BLOCKS, one)

    for h in range(2):
        wait(rs_rcv[h], rs.at[BACK_SPREAD + h])
        wait(ret0[h], rs.at[BACK_FIRST + h])
        finish(h)
    wait(outv, ls.at[OUT])

    wait(snd0.at[pl.ds(0, NF - 1)], ss.at[FIRST])
    for h in range(2):
        wait(ret0[h].at[pl.ds(0, NF - 1)], ss.at[BACK_FIRST + h])
        for phase in (SPREAD, CROSS, BACK_CROSS, BACK_SPREAD):
            wait(sp_snd[h].at[pl.ds(0, (NT - 1) * SECONDS)], ss.at[phase + h])
        for phase in (COLLECT, BACK_COLLECT):
            wait(c_snd[h].at[pl.ds(0, PAIRS - 1)], ss.at[phase + h])
    wait(ids_all.at[pl.ds(0, NT - 1)], ss.at[IDS])
    wait(sum_f.at[pl.ds(0, NF - 1)], ss.at[SUM_F])
    wait(sum_t.at[pl.ds(0, NT - 1)], ss.at[SUM_T])


def packed(gradient, slot_ids, left_root, right_root):
    piece = (pltpu.VMEM((NT * SECONDS, HALF, CW), BF16),) * 2
    matrix = pltpu.VMEM((W, W), BF16)
    rows = pltpu.VMEM((NF, ROWS, W), BF16)
    columns = pltpu.VMEM((NT, NF, 2, HALF, CW), BF16)
    plane = (pltpu.VMEM((PAIRS, NZ, HALF, CW), BF16),) * 2
    roots = pltpu.VMEM((2, W, W), BF16)
    return pl.pallas_call(
        kernel,
        out_shape=(
            jax.ShapeDtypeStruct((BLOCKS, ROWS, W), BF16),
            jax.ShapeDtypeStruct((1, 1), I32),
        ),
        in_specs=[
            pl.BlockSpec(memory_space=pltpu.VMEM),
            pl.BlockSpec(memory_space=pltpu.SMEM),
            pl.BlockSpec(memory_space=pl.ANY),
            pl.BlockSpec(memory_space=pl.ANY),
            pl.BlockSpec(memory_space=pl.ANY),
        ],
        out_specs=(pl.BlockSpec(memory_space=pl.ANY), pl.BlockSpec(memory_space=pltpu.SMEM)),
        scratch_shapes=[
            rows,
            roots,
            roots,
            rows,
            matrix,
            piece,
            piece,
            piece,
            piece,
            plane,
            columns,
            pltpu.VMEM((BAND, W), BF16),
            matrix,
            columns,
            (pltpu.VMEM((NF, HALF, W), BF16),) * 2,
            plane,
            piece,
            piece,
            piece,
            piece,
            rows,
            pltpu.VMEM((8, 128), I32),
            pltpu.VMEM((NT, 8, 128), I32),
            pltpu.VMEM((2, 8, 128), I32),
            pltpu.VMEM((N_TABS, 16, 128), I32),
            pltpu.SMEM((2, 8, 128), I32),
            pltpu.SMEM((N_TABS, 16, 128), I32),
            pltpu.VMEM((8, 128), F32),
            pltpu.VMEM((8, 128), F32),
            pltpu.VMEM((NF, 8, 128), F32),
            pltpu.VMEM((NT, 8, 128), F32),
            pltpu.SemaphoreType.DMA((N_SEMS,)),
            pltpu.SemaphoreType.DMA((N_SEMS,)),
            pltpu.SemaphoreType.DMA((N_LOCAL,)),
        ],
        compiler_params=pltpu.CompilerParams(
            collective_id=0, has_side_effects=True, vmem_limit_bytes=56 * 2**20
        ),
    )(slot_ids.reshape(1, BLOCKS), slot_ids, gradient, left_root, right_root)


def plain(gradient, slot_ids, left_root, right_root):
    fsdp_size = lax.axis_size("fsdp")
    tp_size = lax.axis_size("tp")
    slot_count = left_root.shape[0]
    group = gradient.shape[0]
    rows = gradient.shape[1]
    width = gradient.shape[2]
    slot_range = jnp.arange(slot_count, dtype=jnp.int32)
    owner_range = jnp.arange(fsdp_size, dtype=jnp.int32)
    targets = (slot_range[:, None] + slot_count * owner_range[None, :]).reshape(-1)
    select = (slot_ids[None, :] == targets[:, None]).astype(jnp.bfloat16)
    outgoing = jnp.einsum(
        "qb,brc->qrc", select, gradient, preferred_element_type=jnp.float32
    ).astype(jnp.bfloat16)
    outgoing = outgoing.reshape(slot_count, fsdp_size * rows, width)
    owned = lax.all_to_all(outgoing, "fsdp", split_axis=1, concat_axis=1, tiled=True)
    inner = jnp.einsum("sij,sjk->sik", left_root, owned, preferred_element_type=jnp.float32).astype(
        jnp.bfloat16
    )
    direction = jnp.einsum(
        "sij,sjk->sik", inner, right_root, preferred_element_type=jnp.float32
    ).astype(jnp.bfloat16)
    returned = lax.all_to_all(direction, "fsdp", split_axis=1, concat_axis=1, tiled=True)
    returned = returned.reshape(slot_count * fsdp_size, rows, width)
    back = jnp.einsum("qb,qrc->brc", select, returned, preferred_element_type=jnp.float32).astype(
        jnp.bfloat16
    )
    wide_back = back.astype(jnp.float32)
    total = lax.psum(jnp.sum(wide_back * wide_back), ("fsdp", "tp"))
    count = group * tp_size * width * width
    factor = 0.5 / jnp.sqrt(total / count + 1e-06)
    return (wide_back * factor).astype(jnp.bfloat16)


def local(gradient, slot_ids, left_root, right_root):
    update, longest = packed(gradient, slot_ids, left_root, right_root)
    return lax.cond(
        longest[0, 0] > LIST,
        lambda u, *args: plain(*args),
        lambda u, *args: u,
        update, gradient, slot_ids, left_root, right_root,
    )


def solution(mesh):
    placed = (
        P("tp", "fsdp", None),
        P("tp"),
        P(("fsdp", "tp"), None, None),
        P(("fsdp", "tp"), None, None),
    )
    return jax.shard_map(
        local, mesh=mesh, in_specs=placed, out_specs=P("tp", "fsdp", None), check_vma=False
    )
```

```python
import jax
import jax.numpy as jnp
from jax import lax
from jax.experimental import pallas as pl
from jax.experimental.pallas import tpu as pltpu
from jax.sharding import PartitionSpec as P

MESH = pl.DeviceIdType.MESH
NF = 32
NZ = 8
NY = 4
NT = 8
BLOCKS = 32
ROWS = 32
W = 1024
CW = 128
SECONDS = 16
LIST = 16
BAND = 256
HALF = 16
PAIRS = NT * NY
PORTIONS = (1, 6, 12, 18, 24, NF)

BF16 = jnp.bfloat16
F32 = jnp.float32
I32 = jnp.int32

FIRST, IDS, SUM_F, SUM_T = 0, 1, 2, 3
BACK_FIRST, SPREAD, CROSS, COLLECT, BACK_COLLECT, BACK_CROSS, BACK_SPREAD, N_SEMS = range(4, 20, 2)
GRAD, LEFT, RIGHT, TAB_A, TAB_B, OUT, OWN, N_LOCAL = range(8)
T_FIRST, T_SEL, T_HAS1, T_HAS2, T_RANK, T_PLACE, T_SECOND, T_BACK, T_CROSS, T_RETURN, N_TABS = range(11)


def dot(a, b):
    return jnp.dot(a, b, preferred_element_type=F32)


def within(index, size):
    return jnp.clip(index, 0, size - 1)


def owners(ids):
    lane = lax.broadcasted_iota(I32, (8, 128), 1)
    zero = jnp.zeros((8, 128), F32)
    p0, p1, b0, b1 = zero, zero, zero, zero
    for b in range(BLOCKS):
        column = jnp.broadcast_to(ids[:, b : b + 1], (8, 128))
        e0 = jnp.where(column == 2 * lane, 1.0, 0.0)
        e1 = jnp.where(column == 2 * lane + 1, 1.0, 0.0)
        p0, p1 = jnp.maximum(p0, e0), jnp.maximum(p1, e1)
        b0, b1 = b0 + b * e0, b1 + b * e1
    has2 = p0 * p1
    earlier = lax.broadcasted_iota(I32, (128, 128), 0) < lax.broadcasted_iota(I32, (128, 128), 1)
    rank = dot(has2.astype(BF16), jnp.where(earlier, 1.0, 0.0).astype(BF16))
    first = jnp.clip(p0 * b0 + (1.0 - p0) * b1, 0.0, BLOCKS - 1.0)
    return p0, p1, first, b1, has2, rank


def by_rank(has2, rank, value, highest):
    lane = lax.broadcasted_iota(I32, (8, 128), 1)
    table = jnp.zeros((8, 128), F32)
    for j in range(SECONDS):
        found = jnp.sum(jnp.where(rank == float(j), has2 * value, 0.0), axis=1, keepdims=True)
        table = jnp.where(lane == j, jnp.broadcast_to(found, (8, 128)), table)
    return jnp.clip(table, 0.0, float(highest)).astype(I32)


def by_place(has2, place, value, highest):
    row = lax.broadcasted_iota(I32, (16, 128), 0)
    rows = jnp.zeros((16, 128), F32)
    for i in range(LIST):
        found = jnp.sum(jnp.where(place == float(i), has2 * value, 0.0), axis=0, keepdims=True)
        rows = jnp.where(row == i, jnp.broadcast_to(found, (16, 128)), rows)
    source = lax.broadcasted_iota(I32, (128, 128), 0)
    target = lax.broadcasted_iota(I32, (128, 128), 1)
    fold = jnp.where((source % NZ == target) & (source < NF), 1.0, 0.0).astype(BF16)
    return jnp.clip(dot(rows.astype(BF16), fold), 0.0, float(highest)).astype(I32)


def kernel(
    ids_ref, ids_smem, grad_hbm, left_hbm, right_hbm, out_hbm, flag_ref,
    grad, left, right, snd0, rcv0, sp_snd, sp_rcv, z_snd, z_rcv, c_snd, rcv1, inner, dir0, dir1,
    ret0, rc, rz_snd, rz_rcv, rs_snd, rs_rcv, outv, ids_snd, ids_all, tab_a, tab_b, tab_as, tab_bs,
    part_f, part_t, sum_f, sum_t, ss, rs, ls,
):
    f = lax.axis_index("fsdp")
    t = lax.axis_index("tp")
    y, z = f // NZ, f % NZ

    def shifted(k):
        return lax.rem(y + k // NZ, NY) * NZ + lax.rem(z + lax.rem(k, NZ), NZ)

    def tp_shifted(k):
        return lax.rem(t + k, NT)

    def z_shifted(k):
        return lax.rem(z + k, NZ)

    def send(source, target, phase, to_f, to_t):
        pltpu.make_async_remote_copy(
            src_ref=source, dst_ref=target, send_sem=ss.at[phase], recv_sem=rs.at[phase],
            device_id=(to_f, to_t), device_id_type=MESH,
        ).start()

    def own(source, target, phase):
        pltpu.make_async_copy(source, target, rs.at[phase]).start()

    def wait(ref, sem):
        pltpu.make_async_copy(ref, ref, sem).wait()

    def loop(lowest, highest, body):
        def step(k, carry):
            body(k)
            return carry

        lax.fori_loop(lowest, highest, step, 0)

    load_grad = pltpu.make_async_copy(grad_hbm, grad, ls.at[GRAD])
    load_left = pltpu.make_async_copy(left_hbm, left, ls.at[LEFT])
    load_right = pltpu.make_async_copy(right_hbm, right, ls.at[RIGHT])
    load_grad.start()

    barrier = pltpu.get_barrier_semaphore()

    def greet_f(k):
        pl.semaphore_signal(barrier, inc=1, device_id=(shifted(k), t), device_id_type=MESH)

    def greet_t(k):
        pl.semaphore_signal(
            barrier, inc=1, device_id=(lax.rem(y + lax.rem(k, NY), NY) * NZ + z, tp_shifted(k // NY)), device_id_type=MESH
        )

    loop(1, NF, greet_f)
    loop(NY, PAIRS, greet_t)
    load_left.start()
    load_right.start()

    ids_snd[...] = jnp.full((8, 128), -1, I32)
    ids_snd[:, :BLOCKS] = jnp.broadcast_to(ids_ref[...], (8, BLOCKS))
    p0, p1, first, second, has2, rank = owners(ids_snd[...])
    tab_a[0] = first.astype(I32)
    tab_a[1] = by_rank(has2, rank, second, BLOCKS - 1)
    copy_a = pltpu.make_async_copy(tab_a, tab_as, ls.at[TAB_A])
    copy_a.start()
    ids_all[t] = ids_snd[...]

    def send_ids(k):
        send(ids_snd, ids_all.at[t], IDS, f, tp_shifted(k))

    copy_a.wait()
    load_grad.wait()

    def pack_spread(j):
        b = within(tab_as[1, 0, j], BLOCKS)
        for h in range(2):
            for r in range(NT):
                sp_snd[h][r * SECONDS + j] = grad[b, h * HALF : (h + 1) * HALF, r * CW : (r + 1) * CW]

    def spread(source, target, phase, h):
        def one(k):
            to = tp_shifted(k)
            send(source[h].at[pl.ds(to * SECONDS, SECONDS)], target[h].at[pl.ds(t * SECONDS, SECONDS)], phase + h, f, to)

        loop(1, NT, one)
        mine = pl.ds(t * SECONDS, SECONDS)
        own(source[h].at[mine], target[h].at[mine], phase + h)

    def cross(source, target, phase, h):
        def one(k):
            to = z_shifted(k)
            send(source[h].at[pl.ds(to * LIST, LIST)], target[h].at[pl.ds(z * LIST, LIST)], phase + h, y * NZ + to, t)

        loop(1, NZ, one)
        mine = pl.ds(z * LIST, LIST)
        own(source[h].at[mine], target[h].at[mine], phase + h)

    def pack_first(o):
        snd0[o] = grad[within(tab_as[0, 0, o], BLOCKS)]

    def send_first(k):
        to = shifted(k)
        send(snd0.at[to], rcv0.at[pl.ds(f * ROWS, ROWS)], FIRST, to, t)

    def send_portion(i):
        loop(PORTIONS[i], PORTIONS[i + 1], send_first)

    loop(0, SECONDS, pack_spread)
    loop(0, NF, pack_first)
    pl.semaphore_wait(barrier, NF - 1 + PAIRS - NY)
    loop(1, NT, send_ids)
    spread(sp_snd, sp_rcv, SPREAD, 0)
    spread(sp_snd, sp_rcv, SPREAD, 1)
    send_portion(0)

    wait(ids_all.at[pl.ds(0, NT - 1)], rs.at[IDS])
    row = lax.broadcasted_iota(I32, (8, 128), 0)
    ids = jnp.zeros((8, 128), I32)
    for g in range(NT):
        ids = jnp.where(row == g, ids_all[g], ids)
    p0, p1, first, second, has2, rank = owners(ids)
    source = lax.broadcasted_iota(I32, (128, 128), 0)
    target = lax.broadcasted_iota(I32, (128, 128), 1)
    plane = jnp.where((source % NZ == target % NZ) & (source < NF), 1.0, 0.0)
    before = jnp.where(source // NZ < target // NZ, plane, 0.0)
    in_plane = dot(has2.astype(BF16), plane.astype(BF16))
    place = dot(has2.astype(BF16), before.astype(BF16))
    for g in range(NT - 1):
        place = place + jnp.where(row > g, jnp.broadcast_to(in_plane[g : g + 1, :], (8, 128)), 0.0)
    longest = jnp.max(jnp.sum(in_plane, axis=0, keepdims=True), axis=1, keepdims=True)
    flag_ref[0, 0] = jnp.max(longest.astype(I32))
    bounded = jnp.clip(place, 0.0, LIST - 1.0)
    group = row.astype(F32)
    lane = lax.broadcasted_iota(I32, (8, 128), 1)
    tab_b[...] = jnp.zeros_like(tab_b)
    tab_b[T_SEL, :8] = (1.0 - p0).astype(I32)
    tab_b[T_HAS1, :8] = jnp.maximum(p0, p1).astype(I32)
    tab_b[T_HAS2, :8] = has2.astype(I32)
    tab_b[T_RANK, :8] = jnp.clip(rank, 0.0, SECONDS - 1.0).astype(I32)
    tab_b[T_PLACE, :8] = bounded.astype(I32)
    tab_b[T_BACK, :8] = by_rank(has2, rank, (lane % NZ).astype(F32) * LIST + bounded, NZ * LIST - 1)
    tab_b[T_CROSS] = by_place(has2, place, group * SECONDS + rank, NT * SECONDS - 1)
    tab_b[T_RETURN] = by_place(has2, place, group * NY + (lane // NZ).astype(F32), PAIRS - 1)
    copy_b = pltpu.make_async_copy(tab_b, tab_bs, ls.at[TAB_B])
    copy_b.start()
    copy_b.wait()

    def pack_cross(h):
        def one(k):
            z_snd[h][k] = sp_rcv[h][within(tab_bs[T_CROSS, k % LIST, k // LIST], NT * SECONDS)]

        loop(0, NZ * LIST, one)

    for h in range(2):
        wait(sp_rcv[h], rs.at[SPREAD + h])
        pack_cross(h)
        cross(z_snd, z_rcv, CROSS, h)
        send_portion(1 + h)
    own(snd0.at[f], rcv0.at[pl.ds(f * ROWS, ROWS)], FIRST)

    here = t * NY + y

    def pack_collect(h):
        def one(q):
            place_q = within(tab_bs[T_PLACE, q // NY, (q % NY) * NZ + z], LIST)
            for s in range(NZ):
                c_snd[h][q, s] = z_rcv[h][s * LIST + place_q]

        loop(0, PAIRS, one)

    def collect(h):
        def one(k):
            to_t, to_y = tp_shifted(k // NY), lax.rem(y + lax.rem(k, NY), NY)
            send(c_snd[h].at[to_t * NY + to_y], rcv1.at[t, pl.ds(y * NZ, NZ), h], COLLECT + h, to_y * NZ + z, to_t)

        loop(1, PAIRS, one)
        own(c_snd[h].at[here], rcv1.at[t, pl.ds(y * NZ, NZ), h], COLLECT + h)

    for h in range(2):
        wait(z_rcv[h], rs.at[CROSS + h])
        pack_collect(h)
        collect(h)
        send_portion(3 + h)

    load_left.wait()
    load_right.wait()
    wait(rcv1.at[:, :, 0], rs.at[COLLECT])
    wait(rcv1.at[:, :, 1], rs.at[COLLECT + 1])

    def squares(total, part):
        wide = part.astype(F32)
        return total + jnp.sum((wide * wide).reshape(BAND // 8, 8, BAND), axis=0)

    def back_collect(to_y, to_t, h):
        send(dir1.at[to_t, pl.ds(to_y * NZ, NZ), h], rc[h].at[here], BACK_COLLECT + h, to_y * NZ + z, to_t)

    def second_band(k, total):
        to_y = lax.rem(y + k, NY)
        rows = pl.ds(to_y * BAND, BAND)
        lhs = left[1, rows, :]
        for c in range(W // BAND):
            rhs = jnp.concatenate([rcv1[2 * c].reshape(W, CW), rcv1[2 * c + 1].reshape(W, CW)], axis=1)
            inner[:, c * BAND : (c + 1) * BAND] = dot(lhs, rhs).astype(BF16)
        mid = inner[...]
        for c in range(W // BAND):
            part = dot(mid, right[1, :, c * BAND : (c + 1) * BAND]).astype(BF16)
            for i in range(2):
                dir1[2 * c + i, pl.ds(to_y * NZ, NZ)] = part[:, i * CW : (i + 1) * CW].reshape(NZ, 2, HALF, CW)
            total = squares(total, part)
        loop(jnp.where(k == 0, 1, 0), NT, lambda r: back_collect(to_y, tp_shifted(r), 0))
        return total

    zeros = jnp.zeros((8, BAND), F32)
    sum1 = lax.fori_loop(0, NY, second_band, zeros)
    loop(1, PAIRS, lambda k: back_collect(lax.rem(y + lax.rem(k, NY), NY), tp_shifted(k // NY), 1))
    for h in range(2):
        own(dir1.at[t, pl.ds(y * NZ, NZ), h], rc[h].at[here], BACK_COLLECT + h)

    wait(rcv0, rs.at[FIRST])
    which = within(tab_bs[T_SEL, t, f], 2)

    def back_first(k, h):
        to = shifted(k)
        send(dir0.at[pl.ds(to * ROWS + h * HALF, HALF)], ret0[h].at[f], BACK_FIRST + h, to, t)

    def first_band(k, total):
        rows = pl.ds(lax.rem(y + k, NY) * BAND, BAND)
        lhs = left[which, rows, :]
        for c in range(W // BAND):
            inner[:, c * BAND : (c + 1) * BAND] = dot(lhs, rcv0[:, c * BAND : (c + 1) * BAND]).astype(BF16)
        mid = inner[...]
        for c in range(W // BAND):
            part = dot(mid, right[which, :, c * BAND : (c + 1) * BAND]).astype(BF16)
            dir0[rows, c * BAND : (c + 1) * BAND] = part
            total = squares(total, part)
        loop(jnp.where(k == 0, 1, 0), NZ, lambda s: back_first(k * NZ + s, 0))
        return total

    sum0 = lax.fori_loop(0, NY, first_band, zeros)
    for h in range(2):
        own(dir0.at[pl.ds(f * ROWS + h * HALF, HALF)], ret0[h].at[f], BACK_FIRST + h)

    kept = jnp.where(tab_bs[T_HAS1, t, f] > 0, sum0, 0.0) + jnp.where(tab_bs[T_HAS2, t, f] > 0, sum1, 0.0)
    part_f[...] = kept[:, :128] + kept[:, 128:]
    sum_f[f] = part_f[...]
    loop(1, NF, lambda k: send(part_f, sum_f.at[f], SUM_F, shifted(k), t))

    def pack_back_cross(h):
        def one(k):
            rz_snd[h][k] = rc[h][within(tab_bs[T_RETURN, k % LIST, z], PAIRS), k // LIST]

        loop(0, NZ * LIST, one)

    for h in range(2):
        wait(rc[h], rs.at[BACK_COLLECT + h])
        pack_back_cross(h)
        cross(rz_snd, rz_rcv, BACK_CROSS, h)

    loop(1, NF, lambda k: back_first(k, 1))

    wait(sum_f.at[pl.ds(0, NF - 1)], rs.at[SUM_F])
    part_t[...] = jnp.sum(sum_f[...], axis=0)
    sum_t[t] = part_t[...]
    loop(1, NT, lambda k: send(part_t, sum_t.at[t], SUM_T, f, tp_shifted(k)))

    def pack_back_spread(h):
        def one(k):
            rs_snd[h][k] = rz_rcv[h][within(tab_bs[T_BACK, k // SECONDS, k % SECONDS], NZ * LIST)]

        loop(0, NT * SECONDS, one)

    for h in range(2):
        wait(rz_rcv[h], rs.at[BACK_CROSS + h])
        pack_back_spread(h)
        spread(rs_snd, rs_rcv, BACK_SPREAD, h)

    wait(sum_t.at[pl.ds(0, NT - 1)], rs.at[SUM_T])
    total = jnp.full((8, 128), jnp.sum(jnp.sum(sum_t[...], axis=0)))
    factor = 0.5 / jnp.sqrt(total / float(NT * BLOCKS * W * W) + 1e-6)
    scale = jnp.broadcast_to(factor[:1, :], (HALF, CW))

    def finish(h):
        def one(b):
            v = within(ids_smem[b], 2 * NF)
            o = v // 2
            is_second = (v % 2) * tab_bs[T_HAS2, t, o]
            j = within(is_second * tab_bs[T_RANK, t, o], SECONDS)
            rows = slice(h * HALF, (h + 1) * HALF)
            for r in range(NT):
                columns = slice(r * CW, (r + 1) * CW)
                value = jnp.where(is_second > 0, rs_rcv[h][r * SECONDS + j], ret0[h][o, :, columns])
                outv[b, rows, columns] = (value.astype(F32) * scale).astype(BF16)
            pltpu.make_async_copy(outv.at[b, rows], out_hbm.at[b, rows], ls.at[OUT]).start()

        loop(0, BLOCKS, one)

    for h in range(2):
        wait(rs_rcv[h], rs.at[BACK_SPREAD + h])
        wait(ret0[h], rs.at[BACK_FIRST + h])
        finish(h)
    wait(outv, ls.at[OUT])

    wait(snd0.at[pl.ds(0, NF - 1)], ss.at[FIRST])
    for h in range(2):
        wait(ret0[h].at[pl.ds(0, NF - 1)], ss.at[BACK_FIRST + h])
        for phase in (SPREAD, CROSS, BACK_CROSS, BACK_SPREAD):
            wait(sp_snd[h].at[pl.ds(0, (NT - 1) * SECONDS)], ss.at[phase + h])
        for phase in (COLLECT, BACK_COLLECT):
            wait(c_snd[h].at[pl.ds(0, PAIRS - 1)], ss.at[phase + h])
    wait(ids_all.at[pl.ds(0, NT - 1)], ss.at[IDS])
    wait(sum_f.at[pl.ds(0, NF - 1)], ss.at[SUM_F])
    wait(sum_t.at[pl.ds(0, NT - 1)], ss.at[SUM_T])


def packed(gradient, slot_ids, left_root, right_root):
    piece = (pltpu.VMEM((NT * SECONDS, HALF, CW), BF16),) * 2
    matrix = pltpu.VMEM((W, W), BF16)
    rows = pltpu.VMEM((NF, ROWS, W), BF16)
    columns = pltpu.VMEM((NT, NF, 2, HALF, CW), BF16)
    plane = (pltpu.VMEM((PAIRS, NZ, HALF, CW), BF16),) * 2
    roots = pltpu.VMEM((2, W, W), BF16)
    return pl.pallas_call(
        kernel,
        out_shape=(
            jax.ShapeDtypeStruct((BLOCKS, ROWS, W), BF16),
            jax.ShapeDtypeStruct((1, 1), I32),
        ),
        in_specs=[
            pl.BlockSpec(memory_space=pltpu.VMEM),
            pl.BlockSpec(memory_space=pltpu.SMEM),
            pl.BlockSpec(memory_space=pl.ANY),
            pl.BlockSpec(memory_space=pl.ANY),
            pl.BlockSpec(memory_space=pl.ANY),
        ],
        out_specs=(pl.BlockSpec(memory_space=pl.ANY), pl.BlockSpec(memory_space=pltpu.SMEM)),
        scratch_shapes=[
            rows,
            roots,
            roots,
            rows,
            matrix,
            piece,
            piece,
            piece,
            piece,
            plane,
            columns,
            pltpu.VMEM((BAND, W), BF16),
            matrix,
            columns,
            (pltpu.VMEM((NF, HALF, W), BF16),) * 2,
            plane,
            piece,
            piece,
            piece,
            piece,
            rows,
            pltpu.VMEM((8, 128), I32),
            pltpu.VMEM((NT, 8, 128), I32),
            pltpu.VMEM((2, 8, 128), I32),
            pltpu.VMEM((N_TABS, 16, 128), I32),
            pltpu.SMEM((2, 8, 128), I32),
            pltpu.SMEM((N_TABS, 16, 128), I32),
            pltpu.VMEM((8, 128), F32),
            pltpu.VMEM((8, 128), F32),
            pltpu.VMEM((NF, 8, 128), F32),
            pltpu.VMEM((NT, 8, 128), F32),
            pltpu.SemaphoreType.DMA((N_SEMS,)),
            pltpu.SemaphoreType.DMA((N_SEMS,)),
            pltpu.SemaphoreType.DMA((N_LOCAL,)),
        ],
        compiler_params=pltpu.CompilerParams(
            collective_id=0, has_side_effects=True, vmem_limit_bytes=56 * 2**20
        ),
    )(slot_ids.reshape(1, BLOCKS), slot_ids, gradient, left_root, right_root)


def plain(gradient, slot_ids, left_root, right_root):
    fsdp_size = lax.axis_size("fsdp")
    tp_size = lax.axis_size("tp")
    slot_count = left_root.shape[0]
    group = gradient.shape[0]
    rows = gradient.shape[1]
    width = gradient.shape[2]
    slot_range = jnp.arange(slot_count, dtype=jnp.int32)
    owner_range = jnp.arange(fsdp_size, dtype=jnp.int32)
    targets = (slot_range[:, None] + slot_count * owner_range[None, :]).reshape(-1)
    select = (slot_ids[None, :] == targets[:, None]).astype(jnp.bfloat16)
    outgoing = jnp.einsum(
        "qb,brc->qrc", select, gradient, preferred_element_type=jnp.float32
    ).astype(jnp.bfloat16)
    outgoing = outgoing.reshape(slot_count, fsdp_size * rows, width)
    owned = lax.all_to_all(outgoing, "fsdp", split_axis=1, concat_axis=1, tiled=True)
    inner = jnp.einsum("sij,sjk->sik", left_root, owned, preferred_element_type=jnp.float32).astype(
        jnp.bfloat16
    )
    direction = jnp.einsum(
        "sij,sjk->sik", inner, right_root, preferred_element_type=jnp.float32
    ).astype(jnp.bfloat16)
    returned = lax.all_to_all(direction, "fsdp", split_axis=1, concat_axis=1, tiled=True)
    returned = returned.reshape(slot_count * fsdp_size, rows, width)
    back = jnp.einsum("qb,qrc->brc", select, returned, preferred_element_type=jnp.float32).astype(
        jnp.bfloat16
    )
    wide_back = back.astype(jnp.float32)
    total = lax.psum(jnp.sum(wide_back * wide_back), ("fsdp", "tp"))
    count = group * tp_size * width * width
    factor = 0.5 / jnp.sqrt(total / count + 1e-06)
    return (wide_back * factor).astype(jnp.bfloat16)


def local(gradient, slot_ids, left_root, right_root):
    update, longest = packed(gradient, slot_ids, left_root, right_root)
    return lax.cond(
        longest[0, 0] > LIST,
        lambda u, *args: plain(*args),
        lambda u, *args: u,
        update, gradient, slot_ids, left_root, right_root,
    )


def solution(mesh):
    placed = (
        P("tp", "fsdp", None),
        P("tp"),
        P(("fsdp", "tp"), None, None),
        P(("fsdp", "tp"), None, None),
    )
    return jax.shard_map(
        local, mesh=mesh, in_specs=placed, out_specs=P("tp", "fsdp", None), check_vma=False
    )
```

```python
import jax
import jax.numpy as jnp
from jax import lax
from jax.experimental import pallas as pl
from jax.experimental.pallas import tpu as pltpu
from jax.sharding import PartitionSpec as P

MESH = pl.DeviceIdType.MESH
NF = 32
NZ = 8
NY = 4
NT = 8
BLOCKS = 32
ROWS = 32
W = 1024
CW = 128
SECONDS = 16
LIST = 16
BAND = 256
HALF = 16
PAIRS = NT * NY
PORTIONS = (1, 6, 12, 18, 24, NF)

BF16 = jnp.bfloat16
F32 = jnp.float32
I32 = jnp.int32

FIRST, IDS, SUM_F, SUM_T = 0, 1, 2, 3
BACK_FIRST, SPREAD, CROSS, COLLECT, BACK_COLLECT, BACK_CROSS, BACK_SPREAD, N_SEMS = range(4, 20, 2)
GRAD, LEFT, RIGHT, TAB_A, TAB_B, OUT, OWN, N_LOCAL = range(8)
T_FIRST, T_SEL, T_HAS1, T_HAS2, T_RANK, T_PLACE, T_SECOND, T_BACK, T_CROSS, T_RETURN, N_TABS = range(11)


def dot(a, b):
    return jnp.dot(a, b, preferred_element_type=F32)


def within(index, size):
    return jnp.clip(index, 0, size - 1)


def owners(ids):
    lane = lax.broadcasted_iota(I32, (8, 128), 1)
    zero = jnp.zeros((8, 128), F32)
    p0, p1, b0, b1 = zero, zero, zero, zero
    for b in range(BLOCKS):
        column = jnp.broadcast_to(ids[:, b : b + 1], (8, 128))
        e0 = jnp.where(column == 2 * lane, 1.0, 0.0)
        e1 = jnp.where(column == 2 * lane + 1, 1.0, 0.0)
        p0, p1 = jnp.maximum(p0, e0), jnp.maximum(p1, e1)
        b0, b1 = b0 + b * e0, b1 + b * e1
    has2 = p0 * p1
    earlier = lax.broadcasted_iota(I32, (128, 128), 0) < lax.broadcasted_iota(I32, (128, 128), 1)
    rank = dot(has2.astype(BF16), jnp.where(earlier, 1.0, 0.0).astype(BF16))
    first = jnp.clip(p0 * b0 + (1.0 - p0) * b1, 0.0, BLOCKS - 1.0)
    return p0, p1, first, b1, has2, rank


def by_rank(has2, rank, value, highest):
    lane = lax.broadcasted_iota(I32, (8, 128), 1)
    table = jnp.zeros((8, 128), F32)
    for j in range(SECONDS):
        found = jnp.sum(jnp.where(rank == float(j), has2 * value, 0.0), axis=1, keepdims=True)
        table = jnp.where(lane == j, jnp.broadcast_to(found, (8, 128)), table)
    return jnp.clip(table, 0.0, float(highest)).astype(I32)


def by_place(has2, place, value, highest):
    row = lax.broadcasted_iota(I32, (16, 128), 0)
    rows = jnp.zeros((16, 128), F32)
    for i in range(LIST):
        found = jnp.sum(jnp.where(place == float(i), has2 * value, 0.0), axis=0, keepdims=True)
        rows = jnp.where(row == i, jnp.broadcast_to(found, (16, 128)), rows)
    source = lax.broadcasted_iota(I32, (128, 128), 0)
    target = lax.broadcasted_iota(I32, (128, 128), 1)
    fold = jnp.where((source % NZ == target) & (source < NF), 1.0, 0.0).astype(BF16)
    return jnp.clip(dot(rows.astype(BF16), fold), 0.0, float(highest)).astype(I32)


def kernel(
    ids_ref, ids_smem, grad_hbm, left_hbm, right_hbm, out_hbm, flag_ref,
    grad, left, right, snd0, rcv0, sp_snd, sp_rcv, z_snd, z_rcv, c_snd, rcv1, inner, dir0, dir1,
    ret0, rc, rz_snd, rz_rcv, rs_snd, rs_rcv, outv, ids_snd, ids_all, tab_a, tab_b, tab_as, tab_bs,
    part_f, part_t, sum_f, sum_t, ss, rs, ls,
):
    f = lax.axis_index("fsdp")
    t = lax.axis_index("tp")
    y, z = f // NZ, f % NZ

    def both_ways(k, n):
        odd = lax.rem(k, 2)
        return odd * ((k + 1) // 2) + (1 - odd) * (n - k // 2)

    def tp_shifted(k):
        return lax.rem(t + both_ways(k, NT), NT)

    def z_shifted(k):
        return lax.rem(z + both_ways(k, NZ), NZ)

    def shifted(k):
        return lax.rem(y + k // NZ, NY) * NZ + z_shifted(lax.rem(k, NZ))

    def pair(k):
        near = lax.rem(k, NT)
        return tp_shifted(near), lax.rem(y + lax.rem(k // NT + near, NY), NY)

    def send(source, target, phase, to_f, to_t):
        pltpu.make_async_remote_copy(
            src_ref=source, dst_ref=target, send_sem=ss.at[phase], recv_sem=rs.at[phase],
            device_id=(to_f, to_t), device_id_type=MESH,
        ).start()

    def own(source, target, phase):
        pltpu.make_async_copy(source, target, rs.at[phase]).start()

    def wait(ref, sem):
        pltpu.make_async_copy(ref, ref, sem).wait()

    def loop(lowest, highest, body):
        def step(k, carry):
            body(k)
            return carry

        lax.fori_loop(lowest, highest, step, 0)

    load_grad = pltpu.make_async_copy(grad_hbm, grad, ls.at[GRAD])
    load_left = pltpu.make_async_copy(left_hbm, left, ls.at[LEFT])
    load_right = pltpu.make_async_copy(right_hbm, right, ls.at[RIGHT])
    load_grad.start()

    barrier = pltpu.get_barrier_semaphore()

    def greet_f(k):
        pl.semaphore_signal(barrier, inc=1, device_id=(shifted(k), t), device_id_type=MESH)

    def greet_t(k):
        pl.semaphore_signal(
            barrier, inc=1, device_id=(lax.rem(y + lax.rem(k, NY), NY) * NZ + z, tp_shifted(k // NY)), device_id_type=MESH
        )

    loop(1, NF, greet_f)
    loop(NY, PAIRS, greet_t)
    load_left.start()
    load_right.start()

    ids_snd[...] = jnp.full((8, 128), -1, I32)
    ids_snd[:, :BLOCKS] = jnp.broadcast_to(ids_ref[...], (8, BLOCKS))
    p0, p1, first, second, has2, rank = owners(ids_snd[...])
    tab_a[0] = first.astype(I32)
    tab_a[1] = by_rank(has2, rank, second, BLOCKS - 1)
    copy_a = pltpu.make_async_copy(tab_a, tab_as, ls.at[TAB_A])
    copy_a.start()
    ids_all[t] = ids_snd[...]

    def send_ids(k):
        send(ids_snd, ids_all.at[t], IDS, f, tp_shifted(k))

    copy_a.wait()
    load_grad.wait()

    def pack_spread(j):
        b = within(tab_as[1, 0, j], BLOCKS)
        for h in range(2):
            for r in range(NT):
                sp_snd[h][r * SECONDS + j] = grad[b, h * HALF : (h + 1) * HALF, r * CW : (r + 1) * CW]

    def spread(source, target, phase, h):
        def one(k):
            to = tp_shifted(k)
            send(source[h].at[pl.ds(to * SECONDS, SECONDS)], target[h].at[pl.ds(t * SECONDS, SECONDS)], phase + h, f, to)

        loop(1, NT, one)
        mine = pl.ds(t * SECONDS, SECONDS)
        own(source[h].at[mine], target[h].at[mine], phase + h)

    def cross(source, target, phase, h):
        def one(k):
            to = z_shifted(k)
            send(source[h].at[pl.ds(to * LIST, LIST)], target[h].at[pl.ds(z * LIST, LIST)], phase + h, y * NZ + to, t)

        loop(1, NZ, one)
        mine = pl.ds(z * LIST, LIST)
        own(source[h].at[mine], target[h].at[mine], phase + h)

    def pack_first(o):
        snd0[o] = grad[within(tab_as[0, 0, o], BLOCKS)]

    def send_first(k):
        to = shifted(k)
        send(snd0.at[to], rcv0.at[pl.ds(f * ROWS, ROWS)], FIRST, to, t)

    def send_portion(i):
        loop(PORTIONS[i], PORTIONS[i + 1], send_first)

    loop(0, SECONDS, pack_spread)
    loop(0, NF, pack_first)
    pl.semaphore_wait(barrier, NF - 1 + PAIRS - NY)
    loop(1, NT, send_ids)
    spread(sp_snd, sp_rcv, SPREAD, 0)
    spread(sp_snd, sp_rcv, SPREAD, 1)
    send_portion(0)

    wait(ids_all.at[pl.ds(0, NT - 1)], rs.at[IDS])
    row = lax.broadcasted_iota(I32, (8, 128), 0)
    ids = jnp.zeros((8, 128), I32)
    for g in range(NT):
        ids = jnp.where(row == g, ids_all[g], ids)
    p0, p1, first, second, has2, rank = owners(ids)
    source = lax.broadcasted_iota(I32, (128, 128), 0)
    target = lax.broadcasted_iota(I32, (128, 128), 1)
    plane = jnp.where((source % NZ == target % NZ) & (source < NF), 1.0, 0.0)
    before = jnp.where(source // NZ < target // NZ, plane, 0.0)
    in_plane = dot(has2.astype(BF16), plane.astype(BF16))
    place = dot(has2.astype(BF16), before.astype(BF16))
    for g in range(NT - 1):
        place = place + jnp.where(row > g, jnp.broadcast_to(in_plane[g : g + 1, :], (8, 128)), 0.0)
    longest = jnp.max(jnp.sum(in_plane, axis=0, keepdims=True), axis=1, keepdims=True)
    flag_ref[0, 0] = jnp.max(longest.astype(I32))
    bounded = jnp.clip(place, 0.0, LIST - 1.0)
    group = row.astype(F32)
    lane = lax.broadcasted_iota(I32, (8, 128), 1)
    tab_b[...] = jnp.zeros_like(tab_b)
    tab_b[T_SEL, :8] = (1.0 - p0).astype(I32)
    tab_b[T_HAS1, :8] = jnp.maximum(p0, p1).astype(I32)
    tab_b[T_HAS2, :8] = has2.astype(I32)
    tab_b[T_RANK, :8] = jnp.clip(rank, 0.0, SECONDS - 1.0).astype(I32)
    tab_b[T_PLACE, :8] = bounded.astype(I32)
    tab_b[T_BACK, :8] = by_rank(has2, rank, (lane % NZ).astype(F32) * LIST + bounded, NZ * LIST - 1)
    tab_b[T_CROSS] = by_place(has2, place, group * SECONDS + rank, NT * SECONDS - 1)
    tab_b[T_RETURN] = by_place(has2, place, group * NY + (lane // NZ).astype(F32), PAIRS - 1)
    copy_b = pltpu.make_async_copy(tab_b, tab_bs, ls.at[TAB_B])
    copy_b.start()
    copy_b.wait()

    def pack_cross(h):
        def one(k):
            z_snd[h][k] = sp_rcv[h][within(tab_bs[T_CROSS, k % LIST, k // LIST], NT * SECONDS)]

        loop(0, NZ * LIST, one)

    for h in range(2):
        wait(sp_rcv[h], rs.at[SPREAD + h])
        pack_cross(h)
        cross(z_snd, z_rcv, CROSS, h)
        send_portion(1 + h)
    own(snd0.at[f], rcv0.at[pl.ds(f * ROWS, ROWS)], FIRST)

    here = t * NY + y

    def pack_collect(h):
        def one(q):
            place_q = within(tab_bs[T_PLACE, q // NY, (q % NY) * NZ + z], LIST)
            for s in range(NZ):
                c_snd[h][q, s] = z_rcv[h][s * LIST + place_q]

        loop(0, PAIRS, one)

    def collect(h):
        def one(k):
            to_t, to_y = pair(k)
            send(c_snd[h].at[to_t * NY + to_y], rcv1.at[t, pl.ds(y * NZ, NZ), h], COLLECT + h, to_y * NZ + z, to_t)

        loop(1, PAIRS, one)
        own(c_snd[h].at[here], rcv1.at[t, pl.ds(y * NZ, NZ), h], COLLECT + h)

    for h in range(2):
        wait(z_rcv[h], rs.at[CROSS + h])
        pack_collect(h)
        collect(h)
        send_portion(3 + h)

    load_left.wait()
    load_right.wait()
    wait(rcv1.at[:, :, 0], rs.at[COLLECT])
    wait(rcv1.at[:, :, 1], rs.at[COLLECT + 1])

    def squares(total, part):
        wide = part.astype(F32)
        return total + jnp.sum((wide * wide).reshape(BAND // 8, 8, BAND), axis=0)

    def back_collect(to_y, to_t, h):
        send(dir1.at[to_t, pl.ds(to_y * NZ, NZ), h], rc[h].at[here], BACK_COLLECT + h, to_y * NZ + z, to_t)

    def second_band(k, total):
        to_y = lax.rem(y + k, NY)
        rows = pl.ds(to_y * BAND, BAND)
        lhs = left[1, rows, :]
        for c in range(W // BAND):
            rhs = jnp.concatenate([rcv1[2 * c].reshape(W, CW), rcv1[2 * c + 1].reshape(W, CW)], axis=1)
            inner[:, c * BAND : (c + 1) * BAND] = dot(lhs, rhs).astype(BF16)
        mid = inner[...]
        for c in range(W // BAND):
            part = dot(mid, right[1, :, c * BAND : (c + 1) * BAND]).astype(BF16)
            for i in range(2):
                dir1[2 * c + i, pl.ds(to_y * NZ, NZ)] = part[:, i * CW : (i + 1) * CW].reshape(NZ, 2, HALF, CW)
            total = squares(total, part)
        loop(jnp.where(k == 0, 1, 0), NT, lambda r: back_collect(to_y, tp_shifted(r), 0))
        return total

    zeros = jnp.zeros((8, BAND), F32)
    sum1 = lax.fori_loop(0, NY, second_band, zeros)
    loop(1, PAIRS, lambda k: back_collect(pair(k)[1], pair(k)[0], 1))
    for h in range(2):
        own(dir1.at[t, pl.ds(y * NZ, NZ), h], rc[h].at[here], BACK_COLLECT + h)

    wait(rcv0, rs.at[FIRST])
    which = within(tab_bs[T_SEL, t, f], 2)

    def back_first(k, h):
        to = shifted(k)
        send(dir0.at[pl.ds(to * ROWS + h * HALF, HALF)], ret0[h].at[f], BACK_FIRST + h, to, t)

    def first_band(k, total):
        rows = pl.ds(lax.rem(y + k, NY) * BAND, BAND)
        lhs = left[which, rows, :]
        for c in range(W // BAND):
            inner[:, c * BAND : (c + 1) * BAND] = dot(lhs, rcv0[:, c * BAND : (c + 1) * BAND]).astype(BF16)
        mid = inner[...]
        for c in range(W // BAND):
            part = dot(mid, right[which, :, c * BAND : (c + 1) * BAND]).astype(BF16)
            dir0[rows, c * BAND : (c + 1) * BAND] = part
            total = squares(total, part)
        loop(jnp.where(k == 0, 1, 0), NZ, lambda s: back_first(k * NZ + s, 0))
        return total

    sum0 = lax.fori_loop(0, NY, first_band, zeros)
    for h in range(2):
        own(dir0.at[pl.ds(f * ROWS + h * HALF, HALF)], ret0[h].at[f], BACK_FIRST + h)

    kept = jnp.where(tab_bs[T_HAS1, t, f] > 0, sum0, 0.0) + jnp.where(tab_bs[T_HAS2, t, f] > 0, sum1, 0.0)
    part_f[...] = kept[:, :128] + kept[:, 128:]
    sum_f[f] = part_f[...]
    loop(1, NF, lambda k: send(part_f, sum_f.at[f], SUM_F, shifted(k), t))

    def pack_back_cross(h):
        def one(k):
            rz_snd[h][k] = rc[h][within(tab_bs[T_RETURN, k % LIST, z], PAIRS), k // LIST]

        loop(0, NZ * LIST, one)

    for h in range(2):
        wait(rc[h], rs.at[BACK_COLLECT + h])
        pack_back_cross(h)
        cross(rz_snd, rz_rcv, BACK_CROSS, h)

    loop(1, NF, lambda k: back_first(k, 1))

    wait(sum_f.at[pl.ds(0, NF - 1)], rs.at[SUM_F])
    part_t[...] = jnp.sum(sum_f[...], axis=0)
    sum_t[t] = part_t[...]
    loop(1, NT, lambda k: send(part_t, sum_t.at[t], SUM_T, f, tp_shifted(k)))

    def pack_back_spread(h):
        def one(k):
            rs_snd[h][k] = rz_rcv[h][within(tab_bs[T_BACK, k // SECONDS, k % SECONDS], NZ * LIST)]

        loop(0, NT * SECONDS, one)

    for h in range(2):
        wait(rz_rcv[h], rs.at[BACK_CROSS + h])
        pack_back_spread(h)
        spread(rs_snd, rs_rcv, BACK_SPREAD, h)

    wait(sum_t.at[pl.ds(0, NT - 1)], rs.at[SUM_T])
    total = jnp.full((8, 128), jnp.sum(jnp.sum(sum_t[...], axis=0)))
    factor = 0.5 / jnp.sqrt(total / float(NT * BLOCKS * W * W) + 1e-6)
    scale = jnp.broadcast_to(factor[:1, :], (HALF, CW))

    def finish(h):
        def one(b):
            v = within(ids_smem[b], 2 * NF)
            o = v // 2
            is_second = (v % 2) * tab_bs[T_HAS2, t, o]
            j = within(is_second * tab_bs[T_RANK, t, o], SECONDS)
            rows = slice(h * HALF, (h + 1) * HALF)
            for r in range(NT):
                columns = slice(r * CW, (r + 1) * CW)
                value = jnp.where(is_second > 0, rs_rcv[h][r * SECONDS + j], ret0[h][o, :, columns])
                outv[b, rows, columns] = (value.astype(F32) * scale).astype(BF16)
            pltpu.make_async_copy(outv.at[b, rows], out_hbm.at[b, rows], ls.at[OUT]).start()

        loop(0, BLOCKS, one)

    for h in range(2):
        wait(rs_rcv[h], rs.at[BACK_SPREAD + h])
        wait(ret0[h], rs.at[BACK_FIRST + h])
        finish(h)
    wait(outv, ls.at[OUT])

    wait(snd0.at[pl.ds(0, NF - 1)], ss.at[FIRST])
    for h in range(2):
        wait(ret0[h].at[pl.ds(0, NF - 1)], ss.at[BACK_FIRST + h])
        for phase in (SPREAD, CROSS, BACK_CROSS, BACK_SPREAD):
            wait(sp_snd[h].at[pl.ds(0, (NT - 1) * SECONDS)], ss.at[phase + h])
        for phase in (COLLECT, BACK_COLLECT):
            wait(c_snd[h].at[pl.ds(0, PAIRS - 1)], ss.at[phase + h])
    wait(ids_all.at[pl.ds(0, NT - 1)], ss.at[IDS])
    wait(sum_f.at[pl.ds(0, NF - 1)], ss.at[SUM_F])
    wait(sum_t.at[pl.ds(0, NT - 1)], ss.at[SUM_T])


def packed(gradient, slot_ids, left_root, right_root):
    piece = (pltpu.VMEM((NT * SECONDS, HALF, CW), BF16),) * 2
    matrix = pltpu.VMEM((W, W), BF16)
    rows = pltpu.VMEM((NF, ROWS, W), BF16)
    columns = pltpu.VMEM((NT, NF, 2, HALF, CW), BF16)
    plane = (pltpu.VMEM((PAIRS, NZ, HALF, CW), BF16),) * 2
    roots = pltpu.VMEM((2, W, W), BF16)
    return pl.pallas_call(
        kernel,
        out_shape=(
            jax.ShapeDtypeStruct((BLOCKS, ROWS, W), BF16),
            jax.ShapeDtypeStruct((1, 1), I32),
        ),
        in_specs=[
            pl.BlockSpec(memory_space=pltpu.VMEM),
            pl.BlockSpec(memory_space=pltpu.SMEM),
            pl.BlockSpec(memory_space=pl.ANY),
            pl.BlockSpec(memory_space=pl.ANY),
            pl.BlockSpec(memory_space=pl.ANY),
        ],
        out_specs=(pl.BlockSpec(memory_space=pl.ANY), pl.BlockSpec(memory_space=pltpu.SMEM)),
        scratch_shapes=[
            rows,
            roots,
            roots,
            rows,
            matrix,
            piece,
            piece,
            piece,
            piece,
            plane,
            columns,
            pltpu.VMEM((BAND, W), BF16),
            matrix,
            columns,
            (pltpu.VMEM((NF, HALF, W), BF16),) * 2,
            plane,
            piece,
            piece,
            piece,
            piece,
            rows,
            pltpu.VMEM((8, 128), I32),
            pltpu.VMEM((NT, 8, 128), I32),
            pltpu.VMEM((2, 8, 128), I32),
            pltpu.VMEM((N_TABS, 16, 128), I32),
            pltpu.SMEM((2, 8, 128), I32),
            pltpu.SMEM((N_TABS, 16, 128), I32),
            pltpu.VMEM((8, 128), F32),
            pltpu.VMEM((8, 128), F32),
            pltpu.VMEM((NF, 8, 128), F32),
            pltpu.VMEM((NT, 8, 128), F32),
            pltpu.SemaphoreType.DMA((N_SEMS,)),
            pltpu.SemaphoreType.DMA((N_SEMS,)),
            pltpu.SemaphoreType.DMA((N_LOCAL,)),
        ],
        compiler_params=pltpu.CompilerParams(
            collective_id=0, has_side_effects=True, vmem_limit_bytes=56 * 2**20
        ),
    )(slot_ids.reshape(1, BLOCKS), slot_ids, gradient, left_root, right_root)


def plain(gradient, slot_ids, left_root, right_root):
    fsdp_size = lax.axis_size("fsdp")
    tp_size = lax.axis_size("tp")
    slot_count = left_root.shape[0]
    group = gradient.shape[0]
    rows = gradient.shape[1]
    width = gradient.shape[2]
    slot_range = jnp.arange(slot_count, dtype=jnp.int32)
    owner_range = jnp.arange(fsdp_size, dtype=jnp.int32)
    targets = (slot_range[:, None] + slot_count * owner_range[None, :]).reshape(-1)
    select = (slot_ids[None, :] == targets[:, None]).astype(jnp.bfloat16)
    outgoing = jnp.einsum(
        "qb,brc->qrc", select, gradient, preferred_element_type=jnp.float32
    ).astype(jnp.bfloat16)
    outgoing = outgoing.reshape(slot_count, fsdp_size * rows, width)
    owned = lax.all_to_all(outgoing, "fsdp", split_axis=1, concat_axis=1, tiled=True)
    inner = jnp.einsum("sij,sjk->sik", left_root, owned, preferred_element_type=jnp.float32).astype(
        jnp.bfloat16
    )
    direction = jnp.einsum(
        "sij,sjk->sik", inner, right_root, preferred_element_type=jnp.float32
    ).astype(jnp.bfloat16)
    returned = lax.all_to_all(direction, "fsdp", split_axis=1, concat_axis=1, tiled=True)
    returned = returned.reshape(slot_count * fsdp_size, rows, width)
    back = jnp.einsum("qb,qrc->brc", select, returned, preferred_element_type=jnp.float32).astype(
        jnp.bfloat16
    )
    wide_back = back.astype(jnp.float32)
    total = lax.psum(jnp.sum(wide_back * wide_back), ("fsdp", "tp"))
    count = group * tp_size * width * width
    factor = 0.5 / jnp.sqrt(total / count + 1e-06)
    return (wide_back * factor).astype(jnp.bfloat16)


def local(gradient, slot_ids, left_root, right_root):
    update, longest = packed(gradient, slot_ids, left_root, right_root)
    return lax.cond(
        longest[0, 0] > LIST,
        lambda u, *args: plain(*args),
        lambda u, *args: u,
        update, gradient, slot_ids, left_root, right_root,
    )


def solution(mesh):
    placed = (
        P("tp", "fsdp", None),
        P("tp"),
        P(("fsdp", "tp"), None, None),
        P(("fsdp", "tp"), None, None),
    )
    return jax.shard_map(
        local, mesh=mesh, in_specs=placed, out_specs=P("tp", "fsdp", None), check_vma=False
    )
```
